512 devices in a mesh: dp: 8 (over y, core), center: 64 (over x, z).
Axes of the slice: x: 4, y: 4, z: 16, core: 2. Of those that a mesh axis runs over, the one named last changes fastest.
Arguments:
- points: bfloat16 [65536, 256], P(('dp', 'center')), may hold values from -93 to 93, as said below
- centers: bfloat16 [65536, 256], P('center'), may hold values from -4 to 4, as said below
- picks: int32 [32768], P(('dp', 'center')), may hold values from 0 to 127
Outputs:
- new_centers: bfloat16 [65536, 256], P('center')
- mass: float32 [65536], P('center')
The draws below stay inside these ranges and needn't reach their ends.
Inputs may be any that keep to these rules, and one draw needn't show every extreme that they name: `points`: real values, with rows of unlike scale. `centers`: real values of order one.
All inputs are finite; a program needn't handle non-finite values.
Results may differ from the reference program's by a relative error of at most 0.0031.
Values may be sent and summed in bfloat16 or wider, within the bound.
No kernel may reach another device: no remote copies, remote signals or barrier semaphores. Data moves between devices by JAX's collectives and lax.ppermute only.
A program may use at most 64 MiB of HBM per device.

```python
import math
import jax
import jax.numpy as jnp
from jax import lax

WIDTH = 256
CENTERS = 65536
ROWS_DEV = 64
SLAB_DEV = 128
ROWS = 32768
SLAB = 65536


def shared_tables(key):
    base = jax.random.normal(jax.random.fold_in(key, 101), (CENTERS, WIDTH), jnp.float32)
    return jnp.clip(base, -3.5, 3.5)


def draw_centers(key, part):
    base = shared_tables(key)
    return base.astype(jnp.bfloat16)


def drawn_rows(table, key, rows):
    index = jnp.arange(SLAB, dtype=jnp.int32)
    offset = jax.random.randint(jax.random.fold_in(key, 3), (), 0, CENTERS // 2)
    target = 2 * ((index * 7919 + offset) % (CENTERS // 2))
    level = jnp.array([150.0, 250.0, 350.0], jnp.float32)[index // 13 % 3]
    strength = level * 16.0 / WIDTH
    pair_mean = 0.5 * (jnp.take(table, target, axis=0) + jnp.take(table, target + 1, axis=0))
    bound = float(24000 // WIDTH)
    aligned = jnp.clip(strength[:, None] * pair_mean + 0.05 * rows, -bound, bound)
    chosen = (index % 13 == 0)[:, None]
    return (aligned, chosen)


def draw_points(key, part):
    base = shared_tables(key)
    key = jax.random.fold_in(key, 5)
    rows = jnp.clip(jax.random.normal(jax.random.fold_in(key, 1), (SLAB, WIDTH), jnp.float32), -4.0, 4.0)
    table = base
    scale = jnp.exp(jax.random.uniform(jax.random.fold_in(key, 2), (SLAB, 1), jnp.float32, -0.69, 0.69))
    aligned, chosen = drawn_rows(table, key, rows)
    return jnp.where(chosen, aligned, scale * rows).astype(jnp.bfloat16)


def plant(drawn, key, least, top_value):
    longest = drawn.shape.index(max(drawn.shape))
    spots = []
    for shift in (0, 1):
        where = [jax.random.randint(jax.random.fold_in(key, axis), (), 0, length) for axis, length in enumerate(drawn.shape)]
        where[longest] = (where[longest] + shift) % drawn.shape[longest]
        spots.append(tuple(where))
    return drawn.at[spots[0]].set(least).at[spots[1]].set(top_value)


def setup_inputs(seed: int = 0) -> dict:
    key_list = jax.random.split(jax.random.key(seed), 4)
    points = draw_points(jax.random.fold_in(key_list[3], 71), 0)
    centers = draw_centers(jax.random.fold_in(key_list[3], 71), 0)
    picks = plant(jax.random.randint(key_list[2], (ROWS,), 0, SLAB_DEV), jax.random.fold_in(key_list[2], 1), 0, SLAB_DEV - 1).astype(jnp.int32)
    return {"points": points, "centers": centers, "picks": picks}


sigma_sq = 8.0


def reference(points, centers, picks):
    owner = jnp.arange(ROWS, dtype=jnp.int32) // ROWS_DEV
    batch = jnp.take(points, owner * SLAB_DEV + picks.astype(jnp.int32), axis=0)
    cen = centers.astype(jnp.float32)
    half_norm = 0.5 * jnp.sum(cen * cen, axis=1)
    block = math.gcd(ROWS, 512)
    blocks = batch.reshape(ROWS // block, block, WIDTH)

    def step(carry, rows):
        weighted, counts = carry
        rows_f = rows.astype(jnp.float32)
        score = (lax.dot_general(rows_f, cen, (((1,), (1,)), ((), ())), precision=lax.Precision.HIGHEST) - half_norm) / sigma_sq
        top = jnp.max(score, axis=1, keepdims=True)
        expo = jnp.exp(score - top)
        resp = expo / jnp.sum(expo, axis=1, keepdims=True)
        resp_low = lax.optimization_barrier(resp.astype(jnp.bfloat16)).astype(jnp.float32)
        weighted = weighted + lax.dot_general(resp_low, rows_f, (((0,), (0,)), ((), ())), precision=lax.Precision.HIGHEST)
        counts = counts + jnp.sum(resp, axis=0)
        return (weighted, counts), None

    init = (jnp.zeros((CENTERS, WIDTH), jnp.float32), jnp.zeros((CENTERS,), jnp.float32))
    (weighted, counts), _ = lax.scan(step, init, blocks)
    new_centers = ((weighted + cen) / (counts[:, None] + 1.0)).astype(jnp.bfloat16)
    return new_centers, counts
```

```python
import functools

import jax
import jax.numpy as jnp
from jax import lax
from jax.experimental import pallas as pl
from jax.experimental.pallas import tpu as pltpu
from jax.sharding import Mesh, PartitionSpec as P

WIDTH = 256
SUB = 256
BLOCK = 1024
LANES = 128
F32 = jnp.float32
BF16 = jnp.bfloat16


def prepare_centers(c_ref, cs_ref, hn_ref):
    c = c_ref[...].astype(F32)
    norm = jnp.sum(c * c, axis=1, keepdims=True) * (1.0 / 16.0)
    hn_ref[...] = jnp.broadcast_to(norm, hn_ref.shape)
    cs_ref[...] = (c * 0.125).astype(BF16)


def scores(cs, hn, rows):
    dots = lax.dot_general(cs, rows, (((1,), (1,)), ((), ())), preferred_element_type=F32)
    return dots - jnp.concatenate([hn] * (rows.shape[0] // LANES), axis=1)


def stats_kernel(rows_ref, c_ref, l_ref, cs_ref, hn_ref):
    @pl.when(pl.program_id(0) == 0)
    def _():
        prepare_centers(c_ref, cs_ref, hn_ref)

    for j in range(BLOCK // SUB):
        s = scores(cs_ref[...], hn_ref[...], rows_ref[j * SUB : (j + 1) * SUB, :])
        top = jnp.max(s, axis=0, keepdims=True)
        lse = top + jnp.log(jnp.sum(jnp.exp(s - top), axis=0, keepdims=True))
        for i in range(SUB // LANES):
            k = j * (SUB // LANES) + i
            l_ref[k : k + 1, :] = lse[:, i * LANES : (i + 1) * LANES]


def row_stats(rows, centers):
    count, k = rows.shape[0], centers.shape[0]
    return pl.pallas_call(
        stats_kernel,
        grid=(count // BLOCK,),
        in_specs=[
            pl.BlockSpec((BLOCK, WIDTH), lambda i: (i, 0)),
            pl.BlockSpec((k, WIDTH), lambda i: (0, 0)),
        ],
        out_specs=pl.BlockSpec((BLOCK // LANES, LANES), lambda i: (i, 0)),
        out_shape=jax.ShapeDtypeStruct((count // LANES, LANES), F32),
        scratch_shapes=[pltpu.VMEM((k, WIDTH), BF16), pltpu.VMEM((k, LANES), F32)],
        compiler_params=pltpu.CompilerParams(vmem_limit_bytes=40 * 2**20),
        name="row_stats",
    )(rows, centers)


def sums_kernel(parts, rows_ref, c_ref, l_ref, out_ref, cs_ref, hn_ref, acc_ref, mass_ref):
    step = pl.program_id(0)

    @pl.when(step == 0)
    def _():
        prepare_centers(c_ref, cs_ref, hn_ref)
        acc_ref[...] = jnp.zeros_like(acc_ref)
        mass_ref[...] = jnp.zeros_like(mass_ref)

    for j in range(BLOCK // SUB):
        rows = rows_ref[j * SUB : (j + 1) * SUB, :]
        s = scores(cs_ref[...], hn_ref[...], rows)
        n = SUB // LANES
        lse = jnp.concatenate([l_ref[j * n + i : j * n + i + 1, :] for i in range(n)], axis=1)
        resp = jnp.exp(s - lse)
        total = resp[:, :LANES]
        for i in range(1, n):
            total = total + resp[:, i * LANES : (i + 1) * LANES]
        mass_ref[...] += total
        acc_ref[...] += jnp.dot(resp.astype(BF16), rows, preferred_element_type=F32)

    @pl.when(step == pl.num_programs(0) - 1)
    def _():
        k = acc_ref.shape[0] // parts
        out_ref[:, k:, :] = jnp.zeros((parts, 8, WIDTH), F32)
        for p in range(parts):
            out_ref[p, :k, :] = acc_ref[p * k : (p + 1) * k, :]
            mass = jnp.sum(jnp.transpose(mass_ref[p * k : (p + 1) * k, :]), axis=0, keepdims=True)
            lane = (p % 2) * LANES
            for q in range(parts):
                out_ref[q, k + p // 2 : k + p // 2 + 1, lane : lane + LANES] = mass
            out_ref[p, k + 4 : k + 5, :LANES] = mass


def row_sums(rows, centers, lse, parts):
    count, k = rows.shape[0], centers.shape[0]
    out = (parts, k // parts + 8, WIDTH)
    return pl.pallas_call(
        functools.partial(sums_kernel, parts),
        grid=(count // BLOCK,),
        in_specs=[
            pl.BlockSpec((BLOCK, WIDTH), lambda i: (i, 0)),
            pl.BlockSpec((k, WIDTH), lambda i: (0, 0)),
            pl.BlockSpec((BLOCK // LANES, LANES), lambda i: (i, 0)),
        ],
        out_specs=pl.BlockSpec(out, lambda i: (0, 0, 0)),
        out_shape=jax.ShapeDtypeStruct(out, F32),
        scratch_shapes=[
            pltpu.VMEM((k, WIDTH), BF16),
            pltpu.VMEM((k, LANES), F32),
            pltpu.VMEM((k, WIDTH), F32),
            pltpu.VMEM((k, LANES), F32),
        ],
        compiler_params=pltpu.CompilerParams(vmem_limit_bytes=40 * 2**20),
        name="row_sums",
    )(rows, centers, lse)


def finish_kernel(got_ref, c_ref, new_ref, mass_ref):
    k = c_ref.shape[0]
    total = got_ref[0]
    for i in range(1, got_ref.shape[0]):
        total = total + got_ref[i]
    mass_ref[...] = total[k : k + 4, :]
    own = jnp.transpose(jnp.broadcast_to(total[k + 4 : k + 5, :LANES], (LANES, k)))
    own = jnp.concatenate([own] * (WIDTH // LANES), axis=1)
    new_ref[...] = ((total[:k, :] + c_ref[...].astype(F32)) / (own + 1.0)).astype(BF16)


def finish(got, centers):
    k = centers.shape[0]
    return pl.pallas_call(
        finish_kernel,
        out_shape=(
            jax.ShapeDtypeStruct((k, WIDTH), BF16),
            jax.ShapeDtypeStruct((4, WIDTH), F32),
        ),
        compiler_params=pltpu.CompilerParams(vmem_limit_bytes=40 * 2**20),
        name="finish",
    )(got, centers)


def everyone(value, axes, count):
    sent = jnp.broadcast_to(value[None], (count,) + value.shape)
    return lax.all_to_all(sent, axes, 0, 0, tiled=True)


def merge(parts):
    top = jnp.max(parts, axis=0)
    return top + jnp.log(jnp.sum(jnp.exp(parts - top[None]), axis=0))


def body(points, centers, picks):
    chosen = (picks[:, None] == lax.iota(jnp.int32, points.shape[0])[None, :]).astype(BF16)
    rows = jnp.dot(chosen, points, preferred_element_type=F32).astype(BF16)
    rows = everyone(rows, "zh", 4).reshape(-1, WIDTH)
    rows = everyone(rows, "zl", 4).reshape(-1, WIDTH)
    rows = everyone(rows, "x", 4).reshape(-1, WIDTH)
    lse = row_stats(rows, centers)
    lse = merge(everyone(lse, ("x", "zl"), 16))
    lse = merge(everyone(lse, "zh", 4))
    sums = row_sums(rows, centers, lse, 8)
    got = lax.all_to_all(sums, ("y", "core"), 0, 0, tiled=True)
    part = lax.axis_index("y") * 2 + lax.axis_index("core")
    k = centers.shape[0] // 8
    new, mass = finish(got, lax.dynamic_slice_in_dim(centers, part * k, k, 0))
    new = lax.all_gather(new, ("y", "core"), axis=0, tiled=True)
    return (new, mass.reshape(-1))


def solution(mesh):
    axes = ("y", "core", "x", "zh", "zl")
    fine = Mesh(mesh.devices.reshape(4, 2, 4, 4, 4), axes)
    return jax.shard_map(
        body,
        mesh=fine,
        in_specs=(P(axes, None), P(axes[2:], None), P(axes)),
        out_specs=(P(axes[2:], None), P(axes[2:])),
        check_vma=False,
    )
```

```python
import functools

import jax
import jax.numpy as jnp
from jax import lax
from jax.experimental import pallas as pl
from jax.experimental.pallas import tpu as pltpu
from jax.sharding import Mesh, PartitionSpec as P

WIDTH = 256
SUB = 256
LANES = 128
F32 = jnp.float32
BF16 = jnp.bfloat16
AXES = ("y", "core", "x", "zh", "zl")
GROUP = ("core", "x", "zh", "zl")
PARAMS = pltpu.CompilerParams(vmem_limit_bytes=40 * 2**20)


def place(core, x, z):
    return (core * 4 + x) * 16 + z


def mixed_groups():
    along_z = [[place(0, x, 4 * h + i) for i in range(4)] for x in range(4) for h in range(4)]
    along_x = [[place(1, i, z) for i in range(4)] for z in range(16)]
    return along_z + along_x


def mixed_moves(d):
    moves = []
    for x in range(4):
        for z in range(16):
            dz = -d if d == 2 and z % 2 else d
            moves.append((place(0, x, z), place(0, (x + d) % 4, z)))
            moves.append((place(1, x, z), place(1, x, (z + dz) % 16)))
    return moves


def cost(rows, centers, dots):
    return pl.CostEstimate(
        flops=2 * dots * rows * centers * WIDTH,
        bytes_accessed=2 * WIDTH * (rows + centers),
        transcendentals=rows * centers,
    )


def prepared(c):
    c = c.astype(F32)
    norm = jnp.sum(c * c, axis=1, keepdims=True) * (1.0 / 16.0)
    return (c * 0.125).astype(BF16), jnp.broadcast_to(norm, (c.shape[0], LANES))


def scores(cs, hn, rows):
    dots = lax.dot_general(cs, rows, (((1,), (1,)), ((), ())), preferred_element_type=F32)
    return dots - jnp.concatenate([hn] * (rows.shape[0] // LANES), axis=1)


def piece_stats(rows_ref, c_ref, cs_ref, hn_ref):
    cs_ref[...], hn_ref[...] = prepared(c_ref[...])
    out = []
    for j in range(rows_ref.shape[0] // SUB):
        s = scores(cs_ref[...], hn_ref[...], rows_ref[j * SUB : (j + 1) * SUB, :])
        top = jnp.max(s, axis=0, keepdims=True)
        lse = top + jnp.log(jnp.sum(jnp.exp(s - top), axis=0, keepdims=True))
        out += [lse[:, i * LANES : (i + 1) * LANES] for i in range(SUB // LANES)]
    return jnp.concatenate(out, axis=0)


def center_scratch(k):
    return [pltpu.VMEM((k, WIDTH), BF16), pltpu.VMEM((k, LANES), F32)]


def stats_kernel(rows_ref, c_ref, l_ref, cs_ref, hn_ref):
    l_ref[...] = piece_stats(rows_ref, c_ref, cs_ref, hn_ref)


def row_stats(rows, centers):
    n, k = rows.shape[0], centers.shape[0]
    return pl.pallas_call(
        stats_kernel,
        out_shape=jax.ShapeDtypeStruct((n // LANES, LANES), F32),
        scratch_shapes=center_scratch(k),
        compiler_params=PARAMS,
        cost_estimate=cost(n, k, 1),
        name="row_stats",
    )(rows, centers)


def piece_at(me, d):
    return pl.multiple_of(((me + 4 - d) % 4) * 8, 8)


def last_kernel(me_ref, r2_ref, c_ref, l0_ref, l1_ref, l3_ref, out_ref, cs_ref, hn_ref):
    l2 = piece_stats(r2_ref, c_ref, cs_ref, hn_ref)
    pieces = (l0_ref[...], l1_ref[...], l2, l3_ref[...])
    me = me_ref[0]
    for copy in range(out_ref.shape[0]):
        for d in range(4):
            out_ref[copy, pl.ds(piece_at(me, d), 8), :] = pieces[d]


def last_stats(me, r2, centers, l0, l1, l3, copies):
    n = 4 * r2.shape[0]
    smem, vmem = pl.BlockSpec(memory_space=pltpu.SMEM), pl.BlockSpec(memory_space=pltpu.VMEM)
    return pl.pallas_call(
        last_kernel,
        in_specs=[smem] + [vmem] * 5,
        out_shape=jax.ShapeDtypeStruct((copies, n // LANES, LANES), F32),
        scratch_shapes=center_scratch(centers.shape[0]),
        compiler_params=PARAMS,
        cost_estimate=cost(r2.shape[0], centers.shape[0], 1),
        name="last_stats",
    )(me, r2, centers, l0, l1, l3)


def merged(parts_ref):
    top = parts_ref[0]
    for i in range(1, parts_ref.shape[0]):
        top = jnp.maximum(top, parts_ref[i])
    total = jnp.exp(parts_ref[0] - top)
    for i in range(1, parts_ref.shape[0]):
        total = total + jnp.exp(parts_ref[i] - top)
    return top + jnp.log(total)


def merge_kernel(parts_ref, out_ref):
    out_ref[...] = jnp.broadcast_to(merged(parts_ref)[None], out_ref.shape)


def merge(parts, copies):
    return pl.pallas_call(
        merge_kernel,
        out_shape=jax.ShapeDtypeStruct((copies,) + parts.shape[1:], F32),
        compiler_params=PARAMS,
        name="merge",
    )(parts)


def sums_kernel(parts, me_ref, half_ref, r0, r1, r2, r3, c_ref, parts_ref, out_ref, mass_ref, l_ref, cs_ref, hn_ref):
    half, k = out_ref.shape[0] * (out_ref.shape[1] - 8), out_ref.shape[1] - 8
    start = pl.multiple_of(half_ref[0] * half, half)
    cs_ref[...], hn_ref[...] = prepared(c_ref[pl.ds(start, half), :])
    me, n = me_ref[0], SUB // LANES
    l_ref[...] = merged(parts_ref)
    first = True
    for d, ref in enumerate((r0, r1, r2, r3)):
        piece = l_ref[pl.ds(piece_at(me, d), 8), :]
        for j in range(ref.shape[0] // SUB):
            rows = ref[j * SUB : (j + 1) * SUB, :]
            at = j * n
            lse = jnp.concatenate([piece[at + i : at + i + 1, :] for i in range(n)], axis=1)
            resp = jnp.exp(scores(cs_ref[...], hn_ref[...], rows) - lse)
            mass = resp[:, :LANES]
            for i in range(1, n):
                mass = mass + resp[:, i * LANES : (i + 1) * LANES]
            sums = jnp.dot(resp.astype(BF16), rows, preferred_element_type=F32)
            if first:
                mass_ref[...] = mass
                for p in range(parts):
                    out_ref[p, :k, :] = sums[p * k : (p + 1) * k, :]
            else:
                mass_ref[...] += mass
                for p in range(parts):
                    out_ref[p, :k, :] += sums[p * k : (p + 1) * k, :]
            first = False

    out_ref[:, k:, :] = jnp.zeros((parts, 8, WIDTH), F32)
    for p in range(parts):
        mass = jnp.sum(jnp.transpose(mass_ref[p * k : (p + 1) * k, :]), axis=0, keepdims=True)
        lane = (p % 2) * LANES
        for q in range(parts):
            out_ref[q, k + p // 2 : k + p // 2 + 1, lane : lane + LANES] = mass
        out_ref[p, k + 2 : k + 3, :LANES] = mass


def half_sums(me, half, pieces, centers, stats, parts):
    k = centers.shape[0] // 2
    l = stats.shape[1:]
    smem, vmem = pl.BlockSpec(memory_space=pltpu.SMEM), pl.BlockSpec(memory_space=pltpu.VMEM)
    return pl.pallas_call(
        functools.partial(sums_kernel, parts),
        in_specs=[smem] * 2 + [vmem] * 6,
        out_shape=jax.ShapeDtypeStruct((parts, k // parts + 8, WIDTH), F32),
        scratch_shapes=[pltpu.VMEM((k, LANES), F32), pltpu.VMEM(l, F32)] + center_scratch(k),
        compiler_params=PARAMS,
        cost_estimate=cost(l[0] * LANES, k, 2),
        name="half_sums",
    )(me, half, *pieces, centers, stats)


def combine_kernel(y_ref, a_ref, b_ref, *out_refs):
    for d, out_ref in enumerate(out_refs):
        p = (y_ref[0] + d) % 4
        out_ref[...] = a_ref[p] + b_ref[p]


def combine(y, a, b):
    smem, vmem = pl.BlockSpec(memory_space=pltpu.SMEM), pl.BlockSpec(memory_space=pltpu.VMEM)
    return pl.pallas_call(
        combine_kernel,
        in_specs=[smem, vmem, vmem],
        out_shape=[jax.ShapeDtypeStruct(a.shape[1:], F32)] * a.shape[0],
        compiler_params=PARAMS,
        name="combine",
    )(y, a, b)


def finish_kernel(a_ref, b_ref, c_ref, d_ref, centers_ref, new_ref, mass_ref):
    k = centers_ref.shape[0]
    total = (a_ref[...] + b_ref[...]) + (c_ref[...] + d_ref[...])
    mass_ref[...] = total[k : k + 2, :]
    own = jnp.transpose(jnp.broadcast_to(total[k + 2 : k + 3, :LANES], (LANES, k)))
    own = jnp.concatenate([own] * (WIDTH // LANES), axis=1)
    new_ref[...] = ((total[:k, :] + centers_ref[...].astype(F32)) / (own + 1.0)).astype(BF16)


def finish(got, centers):
    k = centers.shape[0]
    return pl.pallas_call(
        finish_kernel,
        out_shape=(
            jax.ShapeDtypeStruct((k, WIDTH), BF16),
            jax.ShapeDtypeStruct((2, WIDTH), F32),
        ),
        compiler_params=PARAMS,
        name="finish",
    )(*got, centers)


def everyone(value, axes, count, groups=None):
    sent = jnp.broadcast_to(value[None], (count,) + value.shape)
    return lax.all_to_all(sent, axes, 0, 0, tiled=True, axis_index_groups=groups)


def around(value, axis, count, d):
    return lax.ppermute(value, axis, [(i, (i + d) % count) for i in range(count)])


def body(points, centers, picks):
    core = lax.axis_index("core").astype(jnp.int32).reshape(1)
    y = lax.axis_index("y").astype(jnp.int32).reshape(1)
    me = jnp.where(core == 0, lax.axis_index("x"), lax.axis_index("zl")).astype(jnp.int32)
    k = centers.shape[0] // 8
    mine = lax.dynamic_slice_in_dim(centers, (core[0] * 4 + y[0]) * k, k, 0)

    chosen = (picks[:, None] == lax.iota(jnp.int32, points.shape[0])[None, :]).astype(BF16)
    rows = jnp.dot(chosen, points, preferred_element_type=F32).astype(BF16)
    rows = everyone(rows, "zh", 4).reshape(-1, WIDTH)
    r0 = everyone(rows, GROUP, 4, mixed_groups()).reshape(-1, WIDTH)
    r2 = lax.ppermute(r0, GROUP, mixed_moves(2))
    r1 = lax.ppermute(r0, GROUP, mixed_moves(1))
    r3 = lax.ppermute(r0, GROUP, mixed_moves(-1))

    l0, l1, l3 = row_stats(r0, centers), row_stats(r1, centers), row_stats(r3, centers)
    stats = last_stats(me, r2, centers, l0, l1, l3, 4)
    stats = lax.all_to_all(stats, "x", 0, 0, tiled=True)
    stats = lax.all_to_all(merge(stats, 16), ("zh", "zl"), 0, 0, tiled=True)

    pieces = (r0, r1, r2, r3)
    theirs = half_sums(me, 1 - core, pieces, centers, stats, 4)
    theirs = around(theirs, "core", 2, 1)
    sums = combine(y, half_sums(me, core, pieces, centers, stats, 4), theirs)
    got = [sums[0]] + [around(sums[d], "y", 4, d) for d in (2, 1, 3)]
    new, mass = finish(got, mine)
    new = lax.all_gather(new, "y", axis=0, tiled=True)
    new = lax.all_gather(new, "core", axis=0, tiled=True)
    mass = lax.all_gather(mass, "core", axis=0, tiled=True)
    return (new, mass.reshape(-1))


def solution(mesh):
    fine = Mesh(mesh.devices.reshape(4, 2, 4, 4, 4), AXES)
    return jax.shard_map(
        body,
        mesh=fine,
        in_specs=(P(AXES, None), P(AXES[2:], None), P(AXES)),
        out_specs=(P(AXES[2:], None), P(AXES[2:])),
        check_vma=False,
    )
```

```python
import functools

import jax
import jax.numpy as jnp
from jax import lax
from jax.experimental import pallas as pl
from jax.experimental.pallas import tpu as pltpu
from jax.sharding import Mesh, PartitionSpec as P

WIDTH = 256
SUB = 256
STEP = 512
LANES = 128
F32 = jnp.float32
BF16 = jnp.bfloat16
AXES = ("y", "core", "x", "zh", "zl")
GROUP = ("core", "x", "zh", "zl")
PARAMS = pltpu.CompilerParams(vmem_limit_bytes=40 * 2**20)


def place(core, x, z):
    return (core * 4 + x) * 16 + z


def mixed_groups():
    along_x = [[place(0, i, z) for i in range(4)] for z in range(16)]
    along_z = [[place(1, x, 4 * h + i) for i in range(4)] for x in range(4) for h in range(4)]
    return along_x + along_z


def mixed_moves(d):
    moves = []
    for x in range(4):
        for z in range(16):
            dz = -d if d == 2 and z % 2 else d
            moves.append((place(0, x, z), place(0, x, (z + dz) % 16)))
            moves.append((place(1, x, z), place(1, (x + d) % 4, z)))
    return moves


def cost(rows, centers, dots):
    return pl.CostEstimate(
        flops=2 * dots * rows * centers * WIDTH,
        bytes_accessed=2 * WIDTH * (rows + centers),
        transcendentals=rows * centers,
    )


def prepared(c):
    c = c.astype(F32)
    norm = jnp.sum(c * c, axis=1, keepdims=True) * (1.0 / 16.0)
    return (c * 0.125).astype(BF16), jnp.broadcast_to(norm, (c.shape[0], LANES))


def scores(cs, hn, rows):
    dots = lax.dot_general(cs, rows, (((1,), (1,)), ((), ())), preferred_element_type=F32)
    return dots - jnp.concatenate([hn] * (rows.shape[0] // LANES), axis=1)


def piece_stats(rows_ref, c_ref, cs_ref, hn_ref):
    cs_ref[...], hn_ref[...] = prepared(c_ref[...])
    out = []
    for j in range(rows_ref.shape[0] // SUB):
        s = scores(cs_ref[...], hn_ref[...], rows_ref[j * SUB : (j + 1) * SUB, :])
        top = jnp.max(s, axis=0, keepdims=True)
        lse = top + jnp.log(jnp.sum(jnp.exp(s - top), axis=0, keepdims=True))
        out += [lse[:, i * LANES : (i + 1) * LANES] for i in range(SUB // LANES)]
    return jnp.concatenate(out, axis=0)


def center_scratch(k):
    return [pltpu.VMEM((k, WIDTH), BF16), pltpu.VMEM((k, LANES), F32)]


def stats_kernel(rows_ref, c_ref, l_ref, cs_ref, hn_ref):
    l_ref[...] = piece_stats(rows_ref, c_ref, cs_ref, hn_ref)


def row_stats(rows, centers):
    n, k = rows.shape[0], centers.shape[0]
    return pl.pallas_call(
        stats_kernel,
        out_shape=jax.ShapeDtypeStruct((n // LANES, LANES), F32),
        scratch_shapes=center_scratch(k),
        compiler_params=PARAMS,
        cost_estimate=cost(n, k, 1),
        name="row_stats",
    )(rows, centers)


def piece_at(me, d):
    return pl.multiple_of(((me + 4 - d) % 4) * 8, 8)


def last_kernel(me_ref, core_ref, y_ref, r2_ref, c_ref, l0_ref, l1_ref, l3_ref, out_ref, cs_ref, hn_ref):
    l2 = piece_stats(r2_ref, c_ref, cs_ref, hn_ref)
    pieces = (l0_ref[...], l1_ref[...], l2, l3_ref[...])
    me = me_ref[0]
    for copy in range(out_ref.shape[0]):
        for d in range(4):
            out_ref[copy, pl.ds(piece_at(me, d), 8), :] = pieces[d]


def last_stats(ids, r2, centers, l0, l1, l3, copies):
    n = 4 * r2.shape[0]
    smem, vmem = pl.BlockSpec(memory_space=pltpu.SMEM), pl.BlockSpec(memory_space=pltpu.VMEM)
    return pl.pallas_call(
        last_kernel,
        in_specs=[smem] * 3 + [vmem] * 5,
        out_shape=jax.ShapeDtypeStruct((copies, n // LANES, LANES), F32),
        scratch_shapes=center_scratch(centers.shape[0]),
        compiler_params=PARAMS,
        cost_estimate=cost(r2.shape[0], centers.shape[0], 1),
        name="last_stats",
    )(*ids, r2, centers, l0, l1, l3)


def merged(parts_ref):
    top = parts_ref[0]
    for i in range(1, parts_ref.shape[0]):
        top = jnp.maximum(top, parts_ref[i])
    total = jnp.exp(parts_ref[0] - top)
    for i in range(1, parts_ref.shape[0]):
        total = total + jnp.exp(parts_ref[i] - top)
    return top + jnp.log(total)


def merge_kernel(parts_ref, out_ref):
    out_ref[...] = jnp.broadcast_to(merged(parts_ref)[None], out_ref.shape)


def merge(parts, copies):
    return pl.pallas_call(
        merge_kernel,
        out_shape=jax.ShapeDtypeStruct((copies,) + parts.shape[1:], F32),
        compiler_params=PARAMS,
        name="merge",
    )(parts)


def sums_kernel(parts, other, me_ref, core_ref, r0, r1, r2, r3, c_ref, parts_ref, out_ref, mass_ref, l_ref, cs_ref, hn_ref):
    half, k = out_ref.shape[0] * (out_ref.shape[1] - 8), out_ref.shape[1] - 8
    start = pl.multiple_of((1 - core_ref[0] if other else core_ref[0]) * half, half)
    cs_ref[...], hn_ref[...] = prepared(c_ref[pl.ds(start, half), :])
    me, n = me_ref[0], STEP // LANES
    l_ref[...] = merged(parts_ref)
    first = True
    for d, ref in enumerate((r0, r1, r2, r3)):
        piece = l_ref[pl.ds(piece_at(me, d), 8), :]
        for j in range(ref.shape[0] // STEP):
            rows = ref[j * STEP : (j + 1) * STEP, :]
            at = j * n
            lse = jnp.concatenate([piece[at + i : at + i + 1, :] for i in range(n)], axis=1)
            resp = jnp.exp(scores(cs_ref[...], hn_ref[...], rows) - lse)
            mass = resp[:, :LANES]
            for i in range(1, n):
                mass = mass + resp[:, i * LANES : (i + 1) * LANES]
            sums = jnp.dot(resp.astype(BF16), rows, preferred_element_type=F32)
            if first:
                mass_ref[...] = mass
                for p in range(parts):
                    out_ref[p, :k, :] = sums[p * k : (p + 1) * k, :]
            else:
                mass_ref[...] += mass
                for p in range(parts):
                    out_ref[p, :k, :] += sums[p * k : (p + 1) * k, :]
            first = False

    out_ref[:, k:, :] = jnp.zeros((parts, 8, WIDTH), F32)
    for p in range(parts):
        mass = jnp.sum(jnp.transpose(mass_ref[p * k : (p + 1) * k, :]), axis=0, keepdims=True)
        out_ref[p, k : k + 1, :LANES] = mass


def half_sums(ids, other, pieces, centers, stats, parts):
    k = centers.shape[0] // 2
    l = stats.shape[1:]
    smem, vmem = pl.BlockSpec(memory_space=pltpu.SMEM), pl.BlockSpec(memory_space=pltpu.VMEM)
    return pl.pallas_call(
        functools.partial(sums_kernel, parts, other),
        in_specs=[smem] * 2 + [vmem] * 6,
        out_shape=jax.ShapeDtypeStruct((parts, k // parts + 8, WIDTH), F32),
        scratch_shapes=[pltpu.VMEM((k, LANES), F32), pltpu.VMEM(l, F32)] + center_scratch(k),
        compiler_params=PARAMS,
        cost_estimate=cost(l[0] * LANES, k, 2),
        name="half_sums",
    )(*ids[:2], *pieces, centers, stats)


def combine_kernel(a_ref, b_ref, out_ref):
    out_ref[...] = a_ref[...] + b_ref[...]


def combine(a, b):
    return pl.pallas_call(
        combine_kernel,
        out_shape=jax.ShapeDtypeStruct(a.shape, F32),
        compiler_params=PARAMS,
        name="combine",
    )(a, b)


def finish_kernel(core_ref, y_ref, got_ref, centers_ref, out_ref):
    k = got_ref.shape[1] - 8
    centers = centers_ref[pl.ds(pl.multiple_of((core_ref[0] * 4 + y_ref[0]) * k, k), k), :]
    total = got_ref[0]
    for i in range(1, got_ref.shape[0]):
        total = total + got_ref[i]
    mass = total[k : k + 1, :LANES]
    own = jnp.transpose(jnp.broadcast_to(mass, (LANES, k)))
    own = jnp.concatenate([own] * (WIDTH // LANES), axis=1)
    new = ((total[:k, :] + centers.astype(F32)) / (own + 1.0)).astype(BF16)
    high = mass.astype(BF16)
    rest = mass - high.astype(F32)
    middle = rest.astype(BF16)
    low = (rest - middle.astype(F32)).astype(BF16)
    terms = [jnp.concatenate([t.astype(F32)] * (WIDTH // LANES), axis=1) for t in (high, middle, low)]
    terms = jnp.concatenate(terms + [jnp.zeros((13, WIDTH), F32)], axis=0).astype(BF16)
    for copy in range(out_ref.shape[0]):
        out_ref[copy, :k, :] = new
        out_ref[copy, k:, :] = terms


def finish(ids, got, centers, copies):
    k = got.shape[1] - 8
    smem, vmem = pl.BlockSpec(memory_space=pltpu.SMEM), pl.BlockSpec(memory_space=pltpu.VMEM)
    return pl.pallas_call(
        finish_kernel,
        in_specs=[smem, smem, vmem, vmem],
        out_shape=jax.ShapeDtypeStruct((copies, k + 16, WIDTH), BF16),
        compiler_params=PARAMS,
        name="finish",
    )(*ids[1:], got, centers)


def split_kernel(parts_ref, new_ref, mass_ref):
    k = parts_ref.shape[1] - 16
    for p in range(parts_ref.shape[0]):
        new_ref[p * k : (p + 1) * k, :] = parts_ref[p, :k, :]
        terms = parts_ref[p, k:, :LANES].astype(F32)
        mass_ref[p : p + 1, :] = (terms[0:1] + terms[1:2]) + terms[2:3]


def split(parts):
    n, k = parts.shape[0], parts.shape[1] - 16
    return pl.pallas_call(
        split_kernel,
        out_shape=(
            jax.ShapeDtypeStruct((n * k, WIDTH), BF16),
            jax.ShapeDtypeStruct((n, k), F32),
        ),
        compiler_params=PARAMS,
        name="split",
    )(parts)


def everyone(value, axes, count, groups=None):
    sent = jnp.broadcast_to(value[None], (count,) + value.shape)
    return lax.all_to_all(sent, axes, 0, 0, tiled=True, axis_index_groups=groups)


def around(value, axis, count, d):
    return lax.ppermute(value, axis, [(i, (i + d) % count) for i in range(count)])


def body(points, centers, picks):
    core = lax.axis_index("core")
    me = jnp.where(core == 0, lax.axis_index("zl"), lax.axis_index("x"))
    ids = [i.astype(jnp.int32).reshape(1) for i in (me, core, lax.axis_index("y"))]

    chosen = (picks[:, None] == lax.iota(jnp.int32, points.shape[0])[None, :]).astype(BF16)
    rows = jnp.dot(chosen, points, preferred_element_type=F32).astype(BF16)
    rows = everyone(rows, "zh", 4).reshape(-1, WIDTH)
    r0 = everyone(rows, GROUP, 4, mixed_groups()).reshape(-1, WIDTH)
    r2 = lax.ppermute(r0, GROUP, mixed_moves(2))
    r1 = lax.ppermute(r0, GROUP, mixed_moves(1))
    r3 = lax.ppermute(r0, GROUP, mixed_moves(-1))

    l0, l1, l3 = row_stats(r0, centers), row_stats(r1, centers), row_stats(r3, centers)
    stats = last_stats(ids, r2, centers, l0, l1, l3, 16)
    stats = lax.all_to_all(stats, ("x", "zl"), 0, 0, tiled=True)
    stats = lax.all_to_all(merge(stats, 4), "zh", 0, 0, tiled=True)

    pieces = (r0, r1, r2, r3)
    theirs = half_sums(ids, True, pieces, centers, stats, 4)
    theirs = around(theirs, "core", 2, 1)
    sums = combine(half_sums(ids, False, pieces, centers, stats, 4), theirs)
    got = lax.all_to_all(sums, "y", 0, 0, tiled=True)
    new = lax.all_to_all(finish(ids, got, centers, 4), "y", 0, 0, tiled=True)
    new, mass = split(lax.all_gather(new, "core", axis=0, tiled=True))
    return (new, mass.reshape(-1))


def solution(mesh):
    fine = Mesh(mesh.devices.reshape(4, 2, 4, 4, 4), AXES)
    return jax.shard_map(
        body,
        mesh=fine,
        in_specs=(P(AXES, None), P(AXES[2:], None), P(AXES)),
        out_specs=(P(AXES[2:], None), P(AXES[2:])),
        check_vma=False,
    )
```

```python
import functools

import jax
import jax.numpy as jnp
from jax import lax
from jax.experimental import pallas as pl
from jax.experimental.pallas import tpu as pltpu
from jax.sharding import Mesh, PartitionSpec as P

WIDTH = 256
SUB = 256
STEP = 512
LANES = 128
F32 = jnp.float32
BF16 = jnp.bfloat16
AXES = ("y", "core", "x", "zh", "zl")
GROUP = ("core", "x", "zh", "zl")
PARAMS = pltpu.CompilerParams(vmem_limit_bytes=40 * 2**20)


def place(core, x, z):
    return (core * 4 + x) * 16 + z


def mixed_groups(first):
    c = first
    along_x = [[place(c, i, z) for i in range(4)] for z in range(16)]
    along_z = [[place(1 - c, x, 4 * h + i) for i in range(4)] for x in range(4) for h in range(4)]
    return along_x + along_z


def far_groups():
    core0 = [[place(0, x, z) for z in range(16)] for x in range(4)]
    core1 = [[place(1, x, 4 * h + i) for x in range(4) for h in range(4)] for i in range(4)]
    return core0 + core1


def swaps(step):
    out = []
    for x in range(4):
        for z in range(16):
            near = z ^ 1 if step == 0 else (z + 1 if z % 2 else z - 1) % 16
            out.append((place(0, x, z), place(0, x ^ 1 if step == 0 else 3 - x, z)))
            out.append((place(1, x, z), place(1, x, near)))
    return out


def cost(rows, centers, dots):
    return pl.CostEstimate(
        flops=2 * dots * rows * centers * WIDTH,
        bytes_accessed=2 * WIDTH * (rows + centers),
        transcendentals=rows * centers,
    )


def prepared(c):
    c = c.astype(F32)
    norm = jnp.sum(c * c, axis=1, keepdims=True) * (1.0 / 16.0)
    return (c * 0.125).astype(BF16), jnp.broadcast_to(norm, (c.shape[0], LANES))


def scores(cs, hn, rows):
    dots = lax.dot_general(cs, rows, (((1,), (1,)), ((), ())), preferred_element_type=F32)
    return dots - jnp.concatenate([hn] * (rows.shape[0] // LANES), axis=1)


def center_scratch(k):
    return [pltpu.VMEM((k, WIDTH), BF16), pltpu.VMEM((k, LANES), F32)]


def stats_kernel(me_ref, core_ref, y_ref, rows_ref, *refs):
    *chunks, out_ref, cs_ref, hn_ref = refs
    before_ref = chunks.pop(0).at[0] if len(chunks[0].shape) == 3 else None
    k = cs_ref.shape[0] // 2
    if len(chunks) == 1:
        chunks = [chunks[0].at[:k], chunks[0].at[k:]]
    for p, chunk in enumerate(chunks):
        cs_ref[p * k : (p + 1) * k, :], hn_ref[p * k : (p + 1) * k, :] = prepared(chunk[...])
    for j in range(rows_ref.shape[0] // SUB):
        rows = rows_ref[j * SUB : (j + 1) * SUB, :]
        tops, totals = [], []
        for p in range(len(chunks)):
            s = scores(cs_ref[p * k : (p + 1) * k, :], hn_ref[p * k : (p + 1) * k, :], rows)
            tops.append(jnp.max(s, axis=0, keepdims=True))
            totals.append(jnp.sum(jnp.exp(s - tops[-1]), axis=0, keepdims=True))
        n = SUB // LANES
        if before_ref is not None:
            tops.append(jnp.concatenate([before_ref[j * n + i : j * n + i + 1, :] for i in range(n)], axis=1))
            totals.append(jnp.ones_like(tops[-1]))
        top = functools.reduce(jnp.maximum, tops)
        lse = top + jnp.log(sum(c * jnp.exp(t - top) for c, t in zip(totals, tops)))
        for i in range(n):
            at = j * n + i
            row = lse[:, i * LANES : (i + 1) * LANES]
            for copy in range(out_ref.shape[0]):
                out_ref[copy, at : at + 1, :] = row


def row_stats(ids, rows, chunks, copies):
    n, k = rows.shape[0], 2 * chunks[0].shape[0] if len(chunks) == 2 and chunks[0].shape == chunks[1].shape else chunks[-1].shape[0]
    smem, vmem = pl.BlockSpec(memory_space=pltpu.SMEM), pl.BlockSpec(memory_space=pltpu.VMEM)
    return pl.pallas_call(
        stats_kernel,
        in_specs=[smem] * 3 + [vmem] * (1 + len(chunks)),
        out_shape=jax.ShapeDtypeStruct((copies, n // LANES, LANES), F32),
        scratch_shapes=center_scratch(k),
        compiler_params=PARAMS,
        cost_estimate=cost(n, k, 1),
        name="row_stats",
    )(*ids, rows, *chunks)


def merged(parts_ref):
    top = parts_ref[0]
    for i in range(1, parts_ref.shape[0]):
        top = jnp.maximum(top, parts_ref[i])
    total = jnp.exp(parts_ref[0] - top)
    for i in range(1, parts_ref.shape[0]):
        total = total + jnp.exp(parts_ref[i] - top)
    return top + jnp.log(total)


def merge_kernel(parts_ref, out_ref):
    out_ref[...] = jnp.broadcast_to(merged(parts_ref)[None], out_ref.shape)


def merge(parts, copies):
    return pl.pallas_call(
        merge_kernel,
        out_shape=jax.ShapeDtypeStruct((copies,) + parts.shape[1:], F32),
        compiler_params=PARAMS,
        name="merge",
    )(parts)


def sums_kernel(parts, other, me_ref, core_ref, r0, r1, r2, c_ref, lse_ref, out_ref, mass_ref, cs_ref, hn_ref):
    half, k = out_ref.shape[0] * (out_ref.shape[1] - 8), out_ref.shape[1] - 8
    start = pl.multiple_of((1 - core_ref[0] if other else core_ref[0]) * half, half)
    cs_ref[...], hn_ref[...] = prepared(c_ref[pl.ds(start, half), :])
    me, n, m = me_ref[0], STEP // LANES, r0.shape[0]
    flipped = 3 - me
    blocks = (
        (r0, me),
        (r1, me + 1 - 2 * (me % 2)),
        (r2.at[:m], flipped),
        (r2.at[m:], flipped + 1 - 2 * (flipped % 2)),
    )
    first = True
    for ref, fourth in blocks:
        piece = lse_ref[pl.ds(pl.multiple_of(fourth * 8, 8), 8), :]
        for j in range(m // STEP):
            rows = ref[j * STEP : (j + 1) * STEP, :]
            lse = jnp.concatenate([piece[j * n + i : j * n + i + 1, :] for i in range(n)], axis=1)
            resp = jnp.exp(scores(cs_ref[...], hn_ref[...], rows) - lse)
            mass = resp[:, :LANES]
            for i in range(1, n):
                mass = mass + resp[:, i * LANES : (i + 1) * LANES]
            sums = jnp.dot(resp.astype(BF16), rows, preferred_element_type=F32)
            if first:
                mass_ref[...] = mass
                for p in range(parts):
                    out_ref[p, :k, :] = sums[p * k : (p + 1) * k, :]
            else:
                mass_ref[...] += mass
                for p in range(parts):
                    out_ref[p, :k, :] += sums[p * k : (p + 1) * k, :]
            first = False

    out_ref[:, k:, :] = jnp.zeros((parts, 8, WIDTH), F32)
    for p in range(parts):
        mass = jnp.sum(jnp.transpose(mass_ref[p * k : (p + 1) * k, :]), axis=0, keepdims=True)
        out_ref[p, k : k + 1, :LANES] = mass


def half_sums(ids, other, blocks, centers, lse, parts):
    k = centers.shape[0] // 2
    smem, vmem = pl.BlockSpec(memory_space=pltpu.SMEM), pl.BlockSpec(memory_space=pltpu.VMEM)
    return pl.pallas_call(
        functools.partial(sums_kernel, parts, other),
        in_specs=[smem] * 2 + [vmem] * 5,
        out_shape=jax.ShapeDtypeStruct((parts, k // parts + 8, WIDTH), F32),
        scratch_shapes=[pltpu.VMEM((k, LANES), F32)] + center_scratch(k),
        compiler_params=PARAMS,
        cost_estimate=cost(lse.shape[0] * LANES, k, 2),
        name="half_sums",
    )(*ids[:2], *blocks, centers, lse)


def combine_kernel(a_ref, b_ref, out_ref):
    out_ref[...] = a_ref[...] + b_ref[...]


def combine(a, b):
    return pl.pallas_call(
        combine_kernel,
        out_shape=jax.ShapeDtypeStruct(a.shape, F32),
        compiler_params=PARAMS,
        name="combine",
    )(a, b)


def finish_kernel(core_ref, y_ref, got_ref, centers_ref, out_ref):
    k = got_ref.shape[1] - 8
    centers = centers_ref[pl.ds(pl.multiple_of((core_ref[0] * 4 + y_ref[0]) * k, k), k), :]
    total = got_ref[0]
    for i in range(1, got_ref.shape[0]):
        total = total + got_ref[i]
    mass = total[k : k + 1, :LANES]
    own = jnp.transpose(jnp.broadcast_to(mass, (LANES, k)))
    own = jnp.concatenate([own] * (WIDTH // LANES), axis=1)
    new = ((total[:k, :] + centers.astype(F32)) / (own + 1.0)).astype(BF16)
    high = mass.astype(BF16)
    rest = mass - high.astype(F32)
    middle = rest.astype(BF16)
    low = (rest - middle.astype(F32)).astype(BF16)
    terms = [jnp.concatenate([t.astype(F32)] * (WIDTH // LANES), axis=1) for t in (high, middle, low)]
    terms = jnp.concatenate(terms + [jnp.zeros((13, WIDTH), F32)], axis=0).astype(BF16)
    for copy in range(out_ref.shape[0]):
        out_ref[copy, :k, :] = new
        out_ref[copy, k:, :] = terms


def finish(ids, got, centers, copies):
    k = got.shape[1] - 8
    smem, vmem = pl.BlockSpec(memory_space=pltpu.SMEM), pl.BlockSpec(memory_space=pltpu.VMEM)
    return pl.pallas_call(
        finish_kernel,
        in_specs=[smem, smem, vmem, vmem],
        out_shape=jax.ShapeDtypeStruct((copies, k + 16, WIDTH), BF16),
        compiler_params=PARAMS,
        name="finish",
    )(*ids[1:], got, centers)


def split_kernel(parts_ref, new_ref, mass_ref):
    k = parts_ref.shape[1] - 16
    for p in range(parts_ref.shape[0]):
        new_ref[p * k : (p + 1) * k, :] = parts_ref[p, :k, :]
        terms = parts_ref[p, k:, :LANES].astype(F32)
        mass_ref[p : p + 1, :] = (terms[0:1] + terms[1:2]) + terms[2:3]


def split(parts):
    n, k = parts.shape[0], parts.shape[1] - 16
    return pl.pallas_call(
        split_kernel,
        out_shape=(
            jax.ShapeDtypeStruct((n * k, WIDTH), BF16),
            jax.ShapeDtypeStruct((n, k), F32),
        ),
        compiler_params=PARAMS,
        name="split",
    )(parts)


def everyone(value, axes, count, groups=None):
    sent = jnp.broadcast_to(value[None], (count,) + value.shape)
    return lax.all_to_all(sent, axes, 0, 0, tiled=True, axis_index_groups=groups)


def around(value, axis, count, d):
    return lax.ppermute(value, axis, [(i, (i + d) % count) for i in range(count)])


def pair_kernel(a_ref, b_ref, after_ref, pair_ref):
    k = a_ref.shape[0]
    pair_ref[:k, :] = a_ref[...]
    pair_ref[k:, :] = b_ref[...]


def pair_after(a, b, after):
    k = a.shape[0]
    vmem = pl.BlockSpec(memory_space=pltpu.VMEM)
    return pl.pallas_call(
        pair_kernel,
        in_specs=[vmem, vmem, pl.BlockSpec(memory_space=pl.ANY)],
        out_shape=jax.ShapeDtypeStruct((2 * k, WIDTH), BF16),
        compiler_params=PARAMS,
        name="pair_after",
    )(a, b, after)


def near_kernel(rows_ref, a_ref, b_ref, sent_ref, pair_ref):
    k = a_ref.shape[0]
    for copy in range(sent_ref.shape[0]):
        sent_ref[copy] = rows_ref[...]
    pair_ref[:k, :] = a_ref[...]
    pair_ref[k:, :] = b_ref[...]


def copies_and_pair(rows, a, b, copies):
    k = a.shape[0]
    return pl.pallas_call(
        near_kernel,
        out_shape=(
            jax.ShapeDtypeStruct((copies,) + rows.shape, BF16),
            jax.ShapeDtypeStruct((2 * k, WIDTH), BF16),
        ),
        compiler_params=PARAMS,
        name="copies_and_pair",
    )(rows, a, b)


def body(points, centers, picks):
    core = lax.axis_index("core")
    me = jnp.where(core == 0, lax.axis_index("x"), lax.axis_index("zl"))
    ids = [i.astype(jnp.int32).reshape(1) for i in (me, core, lax.axis_index("y"))]

    near = lax.ppermute(centers, GROUP, swaps(0))
    chosen = (picks[:, None] == lax.iota(jnp.int32, points.shape[0])[None, :]).astype(BF16)
    rows = jnp.dot(chosen, points, preferred_element_type=F32).astype(BF16)
    rows = everyone(rows, "zh", 4).reshape(-1, WIDTH)
    rows, pair = copies_and_pair(rows, centers, near, 4)
    across = lax.ppermute(pair, GROUP, swaps(1))
    rows = lax.all_to_all(rows, GROUP, 0, 0, tiled=True, axis_index_groups=mixed_groups(1)).reshape(-1, WIDTH)
    next_rows = lax.ppermute(rows, GROUP, swaps(0))

    stats = row_stats(ids, rows, (centers, near), 1)
    stats = row_stats(ids, rows, (stats, across), 16)
    pair = pair_after(rows, next_rows, stats)
    stats = lax.all_to_all(stats, GROUP, 0, 0, tiled=True, axis_index_groups=far_groups())
    blocks = rows, next_rows, lax.ppermute(pair, GROUP, swaps(1))
    stats = merge(stats, 4)
    lse = lax.all_to_all(stats, GROUP, 0, 0, tiled=True, axis_index_groups=mixed_groups(0)).reshape(-1, LANES)

    theirs = half_sums(ids, True, blocks, centers, lse, 4)
    theirs = around(theirs, "core", 2, 1)
    sums = combine(half_sums(ids, False, blocks, centers, lse, 4), theirs)
    got = lax.all_to_all(sums, "y", 0, 0, tiled=True)
    new = lax.all_to_all(finish(ids, got, centers, 4), "y", 0, 0, tiled=True)
    new, mass = split(lax.all_gather(new, "core", axis=0, tiled=True))
    return (new, mass.reshape(-1))


def solution(mesh):
    fine = Mesh(mesh.devices.reshape(4, 2, 4, 4, 4), AXES)
    return jax.shard_map(
        body,
        mesh=fine,
        in_specs=(P(AXES, None), P(AXES[2:], None), P(AXES)),
        out_specs=(P(AXES[2:], None), P(AXES[2:])),
        check_vma=False,
    )
```

```python
import functools

import jax
import jax.numpy as jnp
from jax import lax
from jax.experimental import pallas as pl
from jax.experimental.pallas import tpu as pltpu
from jax.sharding import Mesh, PartitionSpec as P

WIDTH = 256
SUB = 256
STEP = 512
LANES = 128
F32 = jnp.float32
BF16 = jnp.bfloat16
AXES = ("y", "core", "x", "zh", "zl")
GROUP = ("core", "x", "zh", "zl")
PARAMS = pltpu.CompilerParams(vmem_limit_bytes=40 * 2**20)


def place(core, x, z):
    return (core * 4 + x) * 16 + z


def mixed_groups(first):
    c = first
    along_x = [[place(c, i, z) for i in range(4)] for z in range(16)]
    along_z = [[place(1 - c, x, 4 * h + i) for i in range(4)] for x in range(4) for h in range(4)]
    return along_x + along_z


def far_groups():
    core0 = [[place(0, x, z) for z in range(16)] for x in range(4)]
    core1 = [[place(1, x, 4 * h + i) for x in range(4) for h in range(4)] for i in range(4)]
    return core0 + core1


def swaps(step):
    out = []
    for x in range(4):
        for z in range(16):
            near = (z + 1 if z % 2 else z - 1) % 16 if step else z ^ 1
            out.append((place(0, x, z), place(0, 3 - x if step else x ^ 1, z)))
            out.append((place(1, x, z), place(1, x, near)))
    return out


def cost(rows, centers, dots):
    return pl.CostEstimate(
        flops=2 * dots * rows * centers * WIDTH,
        bytes_accessed=2 * WIDTH * (rows + centers),
        transcendentals=rows * centers,
    )


def prepared(c):
    c = c.astype(F32)
    norm = jnp.sum(c * c, axis=1, keepdims=True) * (1.0 / 16.0)
    return (c * 0.125).astype(BF16), jnp.broadcast_to(norm, (c.shape[0], LANES))


def scores(cs, hn, rows):
    dots = lax.dot_general(cs, rows, (((1,), (1,)), ((), ())), preferred_element_type=F32)
    return dots - jnp.concatenate([hn] * (rows.shape[0] // LANES), axis=1)


def center_scratch(k):
    return [pltpu.VMEM((k, WIDTH), BF16), pltpu.VMEM((k, LANES), F32)]


def stats_kernel(chained, me_ref, core_ref, y_ref, rows_ref, *refs):
    *chunks, out_ref, cs_ref, hn_ref = refs
    before_ref = chunks.pop(0) if chained else None
    k = chunks[0].shape[0]
    for p, chunk in enumerate(chunks):
        cs_ref[p * k : (p + 1) * k, :], hn_ref[p * k : (p + 1) * k, :] = prepared(chunk[...])
    for j in range(rows_ref.shape[0] // SUB):
        rows = rows_ref[j * SUB : (j + 1) * SUB, :]
        tops, totals = [], []
        for p in range(len(chunks)):
            s = scores(cs_ref[p * k : (p + 1) * k, :], hn_ref[p * k : (p + 1) * k, :], rows)
            tops.append(jnp.max(s, axis=0, keepdims=True))
            totals.append(jnp.sum(jnp.exp(s - tops[-1]), axis=0, keepdims=True))
        n = SUB // LANES
        if chained:
            tops.append(jnp.concatenate([before_ref[0, j * n + i : j * n + i + 1, :] for i in range(n)], axis=1))
            totals.append(jnp.ones_like(tops[-1]))
        top = functools.reduce(jnp.maximum, tops)
        lse = top + jnp.log(sum(c * jnp.exp(t - top) for c, t in zip(totals, tops)))
        for i in range(n):
            at = j * n + i
            row = lse[:, i * LANES : (i + 1) * LANES]
            for copy in range(out_ref.shape[0]):
                out_ref[copy, at : at + 1, :] = row


def row_stats(ids, rows, before, chunks, copies=1):
    n, k = rows.shape[0], sum(c.shape[0] for c in chunks)
    smem, vmem = pl.BlockSpec(memory_space=pltpu.SMEM), pl.BlockSpec(memory_space=pltpu.VMEM)
    return pl.pallas_call(
        functools.partial(stats_kernel, bool(before)),
        in_specs=[smem] * 3 + [vmem] * (1 + len(before) + len(chunks)),
        out_shape=jax.ShapeDtypeStruct((copies, n // LANES, LANES), F32),
        scratch_shapes=center_scratch(k),
        compiler_params=PARAMS,
        cost_estimate=cost(n, k, 1),
        name="row_stats",
    )(*ids, rows, *before, *chunks)


def merged(parts_ref):
    top = parts_ref[0]
    for i in range(1, parts_ref.shape[0]):
        top = jnp.maximum(top, parts_ref[i])
    total = jnp.exp(parts_ref[0] - top)
    for i in range(1, parts_ref.shape[0]):
        total = total + jnp.exp(parts_ref[i] - top)
    return top + jnp.log(total)


def merge_kernel(parts_ref, out_ref):
    out_ref[...] = jnp.broadcast_to(merged(parts_ref)[None], out_ref.shape)


def merge(parts, copies):
    return pl.pallas_call(
        merge_kernel,
        out_shape=jax.ShapeDtypeStruct((copies,) + parts.shape[1:], F32),
        compiler_params=PARAMS,
        name="merge",
    )(parts)


def sums_kernel(parts, other, me_ref, core_ref, r0, r1, r2, c_ref, lse_ref, out_ref, mass_ref, cs_ref, hn_ref):
    half, k = out_ref.shape[0] * (out_ref.shape[1] - 8), out_ref.shape[1] - 8
    start = pl.multiple_of((1 - core_ref[0] if other else core_ref[0]) * half, half)
    cs_ref[...], hn_ref[...] = prepared(c_ref[pl.ds(start, half), :])
    me, n, m = me_ref[0], STEP // LANES, r0.shape[0]
    beside = me + 1 - 2 * (me % 2)
    blocks = ((r0, me), (r1, beside), (r2.at[:m], 3 - me), (r2.at[m:], 3 - beside))
    first = True
    for ref, fourth in blocks:
        piece = lse_ref[pl.ds(pl.multiple_of(fourth * 8, 8), 8), :]
        for j in range(m // STEP):
            rows = ref[j * STEP : (j + 1) * STEP, :]
            lse = jnp.concatenate([piece[j * n + i : j * n + i + 1, :] for i in range(n)], axis=1)
            resp = jnp.exp(scores(cs_ref[...], hn_ref[...], rows) - lse)
            mass = resp[:, :LANES]
            for i in range(1, n):
                mass = mass + resp[:, i * LANES : (i + 1) * LANES]
            sums = jnp.dot(resp.astype(BF16), rows, preferred_element_type=F32)
            if first:
                mass_ref[...] = mass
                for p in range(parts):
                    out_ref[p, :k, :] = sums[p * k : (p + 1) * k, :]
            else:
                mass_ref[...] += mass
                for p in range(parts):
                    out_ref[p, :k, :] += sums[p * k : (p + 1) * k, :]
            first = False

    out_ref[:, k:, :] = jnp.zeros((parts, 8, WIDTH), F32)
    for p in range(parts):
        mass = jnp.sum(jnp.transpose(mass_ref[p * k : (p + 1) * k, :]), axis=0, keepdims=True)
        out_ref[p, k : k + 1, :LANES] = mass


def half_sums(ids, other, blocks, centers, lse, parts):
    k = centers.shape[0] // 2
    smem, vmem = pl.BlockSpec(memory_space=pltpu.SMEM), pl.BlockSpec(memory_space=pltpu.VMEM)
    return pl.pallas_call(
        functools.partial(sums_kernel, parts, other),
        in_specs=[smem] * 2 + [vmem] * 5,
        out_shape=jax.ShapeDtypeStruct((parts, k // parts + 8, WIDTH), F32),
        scratch_shapes=[pltpu.VMEM((k, LANES), F32)] + center_scratch(k),
        compiler_params=PARAMS,
        cost_estimate=cost(lse.shape[0] * LANES, k, 2),
        name="half_sums",
    )(*ids[:2], *blocks, centers, lse)


def combine_kernel(a_ref, b_ref, out_ref):
    out_ref[...] = a_ref[...] + b_ref[...]


def combine(a, b):
    return pl.pallas_call(
        combine_kernel,
        out_shape=jax.ShapeDtypeStruct(a.shape, F32),
        compiler_params=PARAMS,
        name="combine",
    )(a, b)


def finish_kernel(core_ref, y_ref, got_ref, centers_ref, out_ref):
    k = got_ref.shape[1] - 8
    centers = centers_ref[pl.ds(pl.multiple_of((core_ref[0] * 4 + y_ref[0]) * k, k), k), :]
    total = got_ref[0]
    for i in range(1, got_ref.shape[0]):
        total = total + got_ref[i]
    mass = total[k : k + 1, :LANES]
    own = jnp.transpose(jnp.broadcast_to(mass, (LANES, k)))
    own = jnp.concatenate([own] * (WIDTH // LANES), axis=1)
    new = ((total[:k, :] + centers.astype(F32)) / (own + 1.0)).astype(BF16)
    high = mass.astype(BF16)
    rest = mass - high.astype(F32)
    middle = rest.astype(BF16)
    low = (rest - middle.astype(F32)).astype(BF16)
    terms = [jnp.concatenate([t.astype(F32)] * (WIDTH // LANES), axis=1) for t in (high, middle, low)]
    terms = jnp.concatenate(terms + [jnp.zeros((13, WIDTH), F32)], axis=0).astype(BF16)
    for copy in range(out_ref.shape[0]):
        out_ref[copy, :k, :] = new
        out_ref[copy, k:, :] = terms


def finish(ids, got, centers, copies):
    k = got.shape[1] - 8
    smem, vmem = pl.BlockSpec(memory_space=pltpu.SMEM), pl.BlockSpec(memory_space=pltpu.VMEM)
    return pl.pallas_call(
        finish_kernel,
        in_specs=[smem, smem, vmem, vmem],
        out_shape=jax.ShapeDtypeStruct((copies, k + 16, WIDTH), BF16),
        compiler_params=PARAMS,
        name="finish",
    )(*ids[1:], got, centers)


def split_kernel(parts_ref, new_ref, mass_ref):
    k = parts_ref.shape[1] - 16
    for p in range(parts_ref.shape[0]):
        new_ref[p * k : (p + 1) * k, :] = parts_ref[p, :k, :]
        terms = parts_ref[p, k:, :LANES].astype(F32)
        mass_ref[p : p + 1, :] = (terms[0:1] + terms[1:2]) + terms[2:3]


def split(parts):
    n, k = parts.shape[0], parts.shape[1] - 16
    return pl.pallas_call(
        split_kernel,
        out_shape=(
            jax.ShapeDtypeStruct((n * k, WIDTH), BF16),
            jax.ShapeDtypeStruct((n, k), F32),
        ),
        compiler_params=PARAMS,
        name="split",
    )(parts)


def everyone(value, axes, count, groups=None):
    sent = jnp.broadcast_to(value[None], (count,) + value.shape)
    return lax.all_to_all(sent, axes, 0, 0, tiled=True, axis_index_groups=groups)


def around(value, axis, count, d):
    return lax.ppermute(value, axis, [(i, (i + d) % count) for i in range(count)])


def pair_kernel(a_ref, b_ref, after_ref, pair_ref):
    k = a_ref.shape[0]
    pair_ref[:k, :] = a_ref[...]
    pair_ref[k:, :] = b_ref[...]


def pair_after(a, b, after):
    k = a.shape[0]
    vmem = pl.BlockSpec(memory_space=pltpu.VMEM)
    return pl.pallas_call(
        pair_kernel,
        in_specs=[vmem, vmem, pl.BlockSpec(memory_space=pl.ANY)],
        out_shape=jax.ShapeDtypeStruct((2 * k, WIDTH), BF16),
        compiler_params=PARAMS,
        name="pair_after",
    )(a, b, after)


def copies_kernel(rows_ref, *refs):
    for copy in range(refs[-1].shape[0]):
        refs[-1][copy] = rows_ref[...]


def copies_after(rows, after, copies):
    vmem = pl.BlockSpec(memory_space=pltpu.VMEM)
    return pl.pallas_call(
        copies_kernel,
        in_specs=[vmem] + [pl.BlockSpec(memory_space=pl.ANY)] * len(after),
        out_shape=jax.ShapeDtypeStruct((copies,) + rows.shape, BF16),
        compiler_params=PARAMS,
        name="copies",
    )(rows, *after)


def body(points, centers, picks):
    core = lax.axis_index("core")
    me = jnp.where(core == 0, lax.axis_index("x"), lax.axis_index("zl"))
    ids = [i.astype(jnp.int32).reshape(1) for i in (me, core, lax.axis_index("y"))]

    near = lax.ppermute(centers, GROUP, swaps(0))
    chosen = (picks[:, None] == lax.iota(jnp.int32, points.shape[0])[None, :]).astype(BF16)
    rows = jnp.dot(chosen, points, preferred_element_type=F32).astype(BF16)
    rows = everyone(rows, "zh", 4).reshape(-1, WIDTH)
    across = [lax.ppermute(c, GROUP, swaps(1)) for c in (centers, near)]
    rows = copies_after(rows, (near,), 4)
    rows = lax.all_to_all(rows, GROUP, 0, 0, tiled=True, axis_index_groups=mixed_groups(1)).reshape(-1, WIDTH)
    next_rows = lax.ppermute(rows, GROUP, swaps(0))

    stats = row_stats(ids, rows, (), (centers, near))
    stats = row_stats(ids, rows, (stats,), across[:1])
    stats = row_stats(ids, rows, (stats,), across[1:], 16)
    pair = pair_after(rows, next_rows, stats)
    stats = lax.all_to_all(stats, GROUP, 0, 0, tiled=True, axis_index_groups=far_groups())
    blocks = rows, next_rows, lax.ppermute(pair, GROUP, swaps(1))
    stats = merge(stats, 4)
    lse = lax.all_to_all(stats, GROUP, 0, 0, tiled=True, axis_index_groups=mixed_groups(0)).reshape(-1, LANES)

    theirs = half_sums(ids, True, blocks, centers, lse, 4)
    theirs = around(theirs, "core", 2, 1)
    sums = combine(half_sums(ids, False, blocks, centers, lse, 4), theirs)
    got = lax.all_to_all(sums, "y", 0, 0, tiled=True)
    new = lax.all_to_all(finish(ids, got, centers, 4), "y", 0, 0, tiled=True)
    new, mass = split(lax.all_gather(new, "core", axis=0, tiled=True))
    return (new, mass.reshape(-1))


def solution(mesh):
    fine = Mesh(mesh.devices.reshape(4, 2, 4, 4, 4), AXES)
    return jax.shard_map(
        body,
        mesh=fine,
        in_specs=(P(AXES, None), P(AXES[2:], None), P(AXES)),
        out_specs=(P(AXES[2:], None), P(AXES[2:])),
        check_vma=False,
    )
```

```python
import functools

import jax
import jax.numpy as jnp
from jax import lax
from jax.experimental import pallas as pl
from jax.experimental.pallas import tpu as pltpu
from jax.sharding import Mesh, PartitionSpec as P

WIDTH = 256
SUB = 256
STEP = 512
LANES = 128
F32 = jnp.float32
BF16 = jnp.bfloat16
AXES = ("y", "core", "x", "zh", "zl")
GROUP = ("core", "x", "zh", "zl")
PARAMS = pltpu.CompilerParams(vmem_limit_bytes=40 * 2**20)


def place(core, x, z):
    return (core * 4 + x) * 16 + z


def mixed_groups(first):
    c = first
    along_x = [[place(c, i, z) for i in range(4)] for z in range(16)]
    along_z = [[place(1 - c, x, 4 * h + i) for i in range(4)] for x in range(4) for h in range(4)]
    return along_x + along_z


def far_groups():
    core0 = [[place(0, x, z) for z in range(16)] for x in range(4)]
    core1 = [[place(1, x, 4 * h + i) for x in range(4) for h in range(4)] for i in range(4)]
    return core0 + core1


def swaps(step):
    out = []
    for x in range(4):
        for z in range(16):
            near = (z + 1 if z % 2 else z - 1) % 16 if step else z ^ 1
            out.append((place(0, x, z), place(0, 3 - x if step else x ^ 1, z)))
            out.append((place(1, x, z), place(1, x, near)))
    return out


def cost(rows, centers, dots):
    return pl.CostEstimate(
        flops=2 * dots * rows * centers * WIDTH,
        bytes_accessed=2 * WIDTH * (rows + centers),
        transcendentals=rows * centers,
    )


def prepared(c):
    c = c.astype(F32)
    norm = jnp.sum(c * c, axis=1, keepdims=True) * (1.0 / 16.0)
    return (c * 0.125).astype(BF16), jnp.broadcast_to(norm, (c.shape[0], LANES))


def scores(cs, hn, rows):
    dots = lax.dot_general(cs, rows, (((1,), (1,)), ((), ())), preferred_element_type=F32)
    return dots - jnp.concatenate([hn] * (rows.shape[0] // LANES), axis=1)


def center_scratch(k):
    return [pltpu.VMEM((k, WIDTH), BF16), pltpu.VMEM((k, LANES), F32)]


def stats_kernel(chained, me_ref, core_ref, y_ref, rows_ref, *refs):
    *chunks, out_ref, cs_ref, hn_ref = refs
    before_ref = chunks.pop(0) if chained else None
    k = chunks[0].shape[0]
    for p, chunk in enumerate(chunks):
        cs_ref[p * k : (p + 1) * k, :], hn_ref[p * k : (p + 1) * k, :] = prepared(chunk[...])
    for j in range(rows_ref.shape[0] // SUB):
        rows = rows_ref[j * SUB : (j + 1) * SUB, :]
        tops, totals = [], []
        for p in range(len(chunks)):
            s = scores(cs_ref[p * k : (p + 1) * k, :], hn_ref[p * k : (p + 1) * k, :], rows)
            tops.append(jnp.max(s, axis=0, keepdims=True))
            totals.append(jnp.sum(jnp.exp(s - tops[-1]), axis=0, keepdims=True))
        n = SUB // LANES
        if chained:
            tops.append(jnp.concatenate([before_ref[0, j * n + i : j * n + i + 1, :] for i in range(n)], axis=1))
            totals.append(jnp.ones_like(tops[-1]))
        top = functools.reduce(jnp.maximum, tops)
        lse = top + jnp.log(sum(c * jnp.exp(t - top) for c, t in zip(totals, tops)))
        for i in range(n):
            at = j * n + i
            row = lse[:, i * LANES : (i + 1) * LANES]
            for copy in range(out_ref.shape[0]):
                out_ref[copy, at : at + 1, :] = row


def row_stats(ids, rows, before, chunks, copies=1):
    n, k = rows.shape[0], sum(c.shape[0] for c in chunks)
    smem, vmem = pl.BlockSpec(memory_space=pltpu.SMEM), pl.BlockSpec(memory_space=pltpu.VMEM)
    return pl.pallas_call(
        functools.partial(stats_kernel, bool(before)),
        in_specs=[smem] * 3 + [vmem] * (1 + len(before) + len(chunks)),
        out_shape=jax.ShapeDtypeStruct((copies, n // LANES, LANES), F32),
        scratch_shapes=center_scratch(k),
        compiler_params=PARAMS,
        cost_estimate=cost(n, k, 1),
        name="row_stats",
    )(*ids, rows, *before, *chunks)


def merged(parts_ref):
    top = parts_ref[0]
    for i in range(1, parts_ref.shape[0]):
        top = jnp.maximum(top, parts_ref[i])
    total = jnp.exp(parts_ref[0] - top)
    for i in range(1, parts_ref.shape[0]):
        total = total + jnp.exp(parts_ref[i] - top)
    return top + jnp.log(total)


def merge_kernel(parts_ref, out_ref):
    out_ref[...] = jnp.broadcast_to(merged(parts_ref)[None], out_ref.shape)


def merge(parts, copies):
    return pl.pallas_call(
        merge_kernel,
        out_shape=jax.ShapeDtypeStruct((copies,) + parts.shape[1:], F32),
        compiler_params=PARAMS,
        cost_estimate=pl.CostEstimate(flops=12 * 10**9, bytes_accessed=10**6, transcendentals=0),
        name="merge",
    )(parts)


def sums_kernel(parts, other, me_ref, core_ref, r0, r1, r2, c_ref, lse_ref, out_ref, mass_ref, cs_ref, hn_ref):
    half, k = out_ref.shape[0] * (out_ref.shape[1] - 8), out_ref.shape[1] - 8
    start = pl.multiple_of((1 - core_ref[0] if other else core_ref[0]) * half, half)
    cs_ref[...], hn_ref[...] = prepared(c_ref[pl.ds(start, half), :])
    me, n, m = me_ref[0], STEP // LANES, r0.shape[0]
    beside = me + 1 - 2 * (me % 2)
    blocks = ((r0, me), (r1, beside), (r2.at[:m], 3 - me), (r2.at[m:], 3 - beside))
    first = True
    for ref, fourth in blocks:
        piece = lse_ref[pl.ds(pl.multiple_of(fourth * 8, 8), 8), :]
        for j in range(m // STEP):
            rows = ref[j * STEP : (j + 1) * STEP, :]
            lse = jnp.concatenate([piece[j * n + i : j * n + i + 1, :] for i in range(n)], axis=1)
            resp = jnp.exp(scores(cs_ref[...], hn_ref[...], rows) - lse)
            mass = resp[:, :LANES]
            for i in range(1, n):
                mass = mass + resp[:, i * LANES : (i + 1) * LANES]
            sums = jnp.dot(resp.astype(BF16), rows, preferred_element_type=F32)
            if first:
                mass_ref[...] = mass
                for p in range(parts):
                    out_ref[p, :k, :] = sums[p * k : (p + 1) * k, :]
            else:
                mass_ref[...] += mass
                for p in range(parts):
                    out_ref[p, :k, :] += sums[p * k : (p + 1) * k, :]
            first = False

    out_ref[:, k:, :] = jnp.zeros((parts, 8, WIDTH), F32)
    for p in range(parts):
        mass = jnp.sum(jnp.transpose(mass_ref[p * k : (p + 1) * k, :]), axis=0, keepdims=True)
        out_ref[p, k : k + 1, :LANES] = mass


def half_sums(ids, other, blocks, centers, lse, parts):
    k = centers.shape[0] // 2
    smem, vmem = pl.BlockSpec(memory_space=pltpu.SMEM), pl.BlockSpec(memory_space=pltpu.VMEM)
    return pl.pallas_call(
        functools.partial(sums_kernel, parts, other),
        in_specs=[smem] * 2 + [vmem] * 5,
        out_shape=jax.ShapeDtypeStruct((parts, k // parts + 8, WIDTH), F32),
        scratch_shapes=[pltpu.VMEM((k, LANES), F32)] + center_scratch(k),
        compiler_params=PARAMS,
        cost_estimate=cost(lse.shape[0] * LANES, k, 2),
        name="half_sums",
    )(*ids[:2], *blocks, centers, lse)


def combine_kernel(a_ref, b_ref, out_ref):
    out_ref[...] = a_ref[...] + b_ref[...]


def combine(a, b):
    return pl.pallas_call(
        combine_kernel,
        out_shape=jax.ShapeDtypeStruct(a.shape, F32),
        compiler_params=PARAMS,
        name="combine",
    )(a, b)


def finish_kernel(core_ref, y_ref, got_ref, centers_ref, out_ref):
    k = got_ref.shape[1] - 8
    centers = centers_ref[pl.ds(pl.multiple_of((core_ref[0] * 4 + y_ref[0]) * k, k), k), :]
    total = got_ref[0]
    for i in range(1, got_ref.shape[0]):
        total = total + got_ref[i]
    mass = total[k : k + 1, :LANES]
    own = jnp.transpose(jnp.broadcast_to(mass, (LANES, k)))
    own = jnp.concatenate([own] * (WIDTH // LANES), axis=1)
    new = ((total[:k, :] + centers.astype(F32)) / (own + 1.0)).astype(BF16)
    high = mass.astype(BF16)
    rest = mass - high.astype(F32)
    middle = rest.astype(BF16)
    low = (rest - middle.astype(F32)).astype(BF16)
    terms = [jnp.concatenate([t.astype(F32)] * (WIDTH // LANES), axis=1) for t in (high, middle, low)]
    terms = jnp.concatenate(terms + [jnp.zeros((13, WIDTH), F32)], axis=0).astype(BF16)
    for copy in range(out_ref.shape[0]):
        out_ref[copy, :k, :] = new
        out_ref[copy, k:, :] = terms


def finish(ids, got, centers, copies):
    k = got.shape[1] - 8
    smem, vmem = pl.BlockSpec(memory_space=pltpu.SMEM), pl.BlockSpec(memory_space=pltpu.VMEM)
    return pl.pallas_call(
        finish_kernel,
        in_specs=[smem, smem, vmem, vmem],
        out_shape=jax.ShapeDtypeStruct((copies, k + 16, WIDTH), BF16),
        compiler_params=PARAMS,
        name="finish",
    )(*ids[1:], got, centers)


def split_kernel(parts_ref, new_ref, mass_ref):
    k = parts_ref.shape[1] - 16
    for p in range(parts_ref.shape[0]):
        new_ref[p * k : (p + 1) * k, :] = parts_ref[p, :k, :]
        terms = parts_ref[p, k:, :LANES].astype(F32)
        mass_ref[p : p + 1, :] = (terms[0:1] + terms[1:2]) + terms[2:3]


def split(parts):
    n, k = parts.shape[0], parts.shape[1] - 16
    return pl.pallas_call(
        split_kernel,
        out_shape=(
            jax.ShapeDtypeStruct((n * k, WIDTH), BF16),
            jax.ShapeDtypeStruct((n, k), F32),
        ),
        compiler_params=PARAMS,
        name="split",
    )(parts)


def everyone(value, axes, count, groups=None):
    sent = jnp.broadcast_to(value[None], (count,) + value.shape)
    return lax.all_to_all(sent, axes, 0, 0, tiled=True, axis_index_groups=groups)


def around(value, axis, count, d):
    return lax.ppermute(value, axis, [(i, (i + d) % count) for i in range(count)])


def pair_kernel(a_ref, b_ref, after_ref, pair_ref):
    k = a_ref.shape[0]
    pair_ref[:k, :] = a_ref[...]
    pair_ref[k:, :] = b_ref[...]


def pair_after(a, b, after):
    k = a.shape[0]
    vmem = pl.BlockSpec(memory_space=pltpu.VMEM)
    return pl.pallas_call(
        pair_kernel,
        in_specs=[vmem, vmem, pl.BlockSpec(memory_space=pl.ANY)],
        out_shape=jax.ShapeDtypeStruct((2 * k, WIDTH), BF16),
        compiler_params=PARAMS,
        name="pair_after",
    )(a, b, after)


def copies_kernel(rows_ref, *refs):
    for copy in range(refs[-1].shape[0]):
        refs[-1][copy] = rows_ref[...]


def copies_after(rows, after, copies):
    vmem = pl.BlockSpec(memory_space=pltpu.VMEM)
    return pl.pallas_call(
        copies_kernel,
        in_specs=[vmem] + [pl.BlockSpec(memory_space=pl.ANY)] * len(after),
        out_shape=jax.ShapeDtypeStruct((copies,) + rows.shape, BF16),
        compiler_params=PARAMS,
        name="copies",
    )(rows, *after)


def body(points, centers, picks):
    core = lax.axis_index("core")
    me = jnp.where(core == 0, lax.axis_index("x"), lax.axis_index("zl"))
    ids = [i.astype(jnp.int32).reshape(1) for i in (me, core, lax.axis_index("y"))]

    near = lax.ppermute(centers, GROUP, swaps(0))
    chosen = (picks[:, None] == lax.iota(jnp.int32, points.shape[0])[None, :]).astype(BF16)
    rows = jnp.dot(chosen, points, preferred_element_type=F32).astype(BF16)
    rows = everyone(rows, "zh", 4).reshape(-1, WIDTH)
    across = [lax.ppermute(c, GROUP, swaps(1)) for c in (centers, near)]
    rows = copies_after(rows, (near,), 4)
    rows = lax.all_to_all(rows, GROUP, 0, 0, tiled=True, axis_index_groups=mixed_groups(1)).reshape(-1, WIDTH)
    next_rows = lax.ppermute(rows, GROUP, swaps(0))

    stats = row_stats(ids, rows, (), (centers, near))
    stats = row_stats(ids, rows, (stats,), across[:1])
    stats = row_stats(ids, rows, (stats,), across[1:], 16)
    pair = pair_after(rows, next_rows, stats)
    stats = lax.all_to_all(stats, GROUP, 0, 0, tiled=True, axis_index_groups=far_groups())
    blocks = rows, next_rows, lax.ppermute(pair, GROUP, swaps(1))
    stats = merge(stats, 4)
    lse = lax.all_to_all(stats, GROUP, 0, 0, tiled=True, axis_index_groups=mixed_groups(0)).reshape(-1, LANES)

    theirs = half_sums(ids, True, blocks, centers, lse, 4)
    theirs = around(theirs, "core", 2, 1)
    sums = combine(half_sums(ids, False, blocks, centers, lse, 4), theirs)
    got = lax.all_to_all(sums, "y", 0, 0, tiled=True)
    new = lax.all_to_all(finish(ids, got, centers, 4), "y", 0, 0, tiled=True)
    new, mass = split(lax.all_gather(new, "core", axis=0, tiled=True))
    return (new, mass.reshape(-1))


def solution(mesh):
    fine = Mesh(mesh.devices.reshape(4, 2, 4, 4, 4), AXES)
    return jax.shard_map(
        body,
        mesh=fine,
        in_specs=(P(AXES, None), P(AXES[2:], None), P(AXES)),
        out_specs=(P(AXES[2:], None), P(AXES[2:])),
        check_vma=False,
    )
```
